768 devices in a mesh: rep: 12 (over z_lo, x), fsdp: 64 (over y, z_hi, core).
Axes of the slice: x: 4, y: 8, z: 12 (z_hi: 4, z_lo: 3; z = z_hi * 3 + z_lo), core: 2. Of those that a mesh axis runs over, the one named last changes fastest.
Arguments:
- global_weights: bfloat16 [6144, 8192], P('fsdp'), as said below
- local_weights: bfloat16 [12, 6144, 8192], P('rep', 'fsdp'), as said below
- outer_momentum: float32 [6144, 8192], P(('fsdp', 'rep')), may hold values from -6 to 6
- outer_step: int32 [12], P('rep'), may hold values from 0 to 49
Outputs:
- new_global: bfloat16 [6144, 8192], P('fsdp')
- new_momentum: float32 [6144, 8192], P(('fsdp', 'rep'))
- mixed_local: bfloat16 [12, 6144, 8192], P('rep', 'fsdp')
The draws below stay inside these ranges and needn't reach their ends.
Inputs may be any that keep to these rules, and one draw needn't show every extreme that they name: Every entry of local_weights[r] - global_weights lies between -1000 and 1000. `global_weights`: weights of order one.
All inputs are finite; a program needn't handle non-finite values.
Results may differ from the reference program's by a relative error of at most 0.0024.
Values may be sent and summed in bfloat16 or wider, within the bound.
No kernel may reach another device: no remote copies, remote signals or barrier semaphores. Data moves between devices by JAX's collectives and lax.ppermute only.
A program may use at most 32 MiB of HBM per device.

```python
import jax
import jax.numpy as jnp
import numpy as np
from jax import lax

D = 8192
BLOCK = 128
ROWS = 6144
REPLICAS = 12


def shared_base(key):
    return jax.random.normal(jax.random.fold_in(key, 11), (ROWS, D), jnp.float32)


def draw_global_weights(key, part):
    weights = shared_base(key)
    return weights.astype(jnp.bfloat16)


def draw_local_weights(key, part):
    weights = shared_base(key)
    key = jax.random.fold_in(key, 2)
    key_rows, key_cols, key_common, key_noise = jax.random.split(key, 4)
    positions = jnp.arange(ROWS, dtype=jnp.float32) / ROWS
    row_scale = jnp.power(10.0, positions) * jnp.exp(jax.random.uniform(key_rows, (ROWS,), jnp.float32, -0.7, 0.7))
    col_scale = jnp.exp(jax.random.uniform(key_cols, (D,), jnp.float32, -0.7, 0.7))
    common = jax.random.normal(key_common, (ROWS, D), jnp.float32)
    noise = jax.random.normal(key_noise, (REPLICAS, ROWS, D), jnp.float32)
    shift = 0.6 * common
    delta = (row_scale[:, None] * col_scale[None, :])[None] * (shift[None] + noise)
    return (weights[None] - delta).astype(jnp.bfloat16)


def with_ends(entries, own_key, low, top_value):
    longest = entries.shape.index(max(entries.shape))
    spots = []
    for shift in (0, 1):
        where = [jax.random.randint(jax.random.fold_in(own_key, axis), (), 0, length) for axis, length in enumerate(entries.shape)]
        where[longest] = (where[longest] + shift) % entries.shape[longest]
        spots.append(tuple(where))
    return entries.at[spots[0]].set(low).at[spots[1]].set(top_value)


def steps_of(stream_key, extent, pieces, least, high):
    factor_of = 1.0
    for position, shards_of in pieces:
        heights = jax.random.uniform(jax.random.fold_in(jax.random.fold_in(stream_key, 6), position), (shards_of,), jnp.float32, least / len(pieces), high / len(pieces))
        factor_of = factor_of * jnp.repeat(jnp.exp(heights), extent[position] // shards_of).reshape((-1,) + (1,) * (len(extent) - 1 - position))
    return factor_of


def normal_values(key, dims, deviation, reach, cuts=(), kind=jnp.bfloat16):
    gain = steps_of(key, dims, cuts, -0.22, 0.18) if cuts else 1.0
    drawn = jax.random.normal(key, dims, jnp.float32) * deviation * gain
    return jnp.minimum(jnp.maximum(drawn, -reach), reach).astype(kind)


def setup_inputs(seed: int = 0) -> dict:
    streams_of = jax.random.split(jax.random.key(seed), 5)
    return {
        "global_weights": draw_global_weights(jax.random.fold_in(streams_of[4], 71), 0),
        "local_weights": draw_local_weights(jax.random.fold_in(streams_of[4], 71), 0),
        "outer_momentum": normal_values(streams_of[2], (ROWS, D), 1.0, 6.0, ((0, 768),), jnp.float32),
        "outer_step": with_ends(jax.random.randint(streams_of[3], (REPLICAS,), 0, 50), jax.random.fold_in(streams_of[3], 1), 0, 49).astype(jnp.int32),
    }


def power_table():
    return jnp.asarray(2.0 ** np.arange(-24, 16), jnp.float32)

def block_scale(blocks):
    largest = lax.optimization_barrier(jnp.max(jnp.abs(blocks), axis=2))
    powers = power_table()
    candidates = jnp.where(powers[None, None, :] >= largest[:, :, None], powers[None, None, :], powers[-1])
    return lax.optimization_barrier(jnp.min(candidates, axis=2))

def quantize(values):
    magnitude = jnp.abs(values)
    rounded = jnp.zeros_like(magnitude)
    for power in range(6, -1, -1):
        threshold = 2.0 ** (-7) if power == 6 else 0.75 * 2.0 ** (-power)
        rounded = jnp.where(magnitude >= threshold, 2.0 ** (-power), rounded)
    return jnp.sign(values) * rounded

def decode_one(global_w, local_one):
    delta = global_w.astype(jnp.float32) - local_one.astype(jnp.float32)
    blocks = delta.reshape(delta.shape[0], D // BLOCK, BLOCK)
    scale = block_scale(blocks)
    codes = quantize(blocks / scale[:, :, None]).astype(jnp.bfloat16)
    decoded = codes.astype(jnp.float32) * scale[:, :, None]
    return decoded.reshape(delta.shape)

def reference(global_weights, local_weights, outer_momentum, outer_step):

    def accumulate(total, local_one):
        return (total + decode_one(global_weights, local_one), None)
    total, unused = lax.scan(accumulate, jnp.zeros((ROWS, D), jnp.float32), local_weights)
    average = total / REPLICAS
    squares = jnp.sum(average * average)
    factor = 0.5 / jnp.sqrt(squares / jnp.float32(ROWS * D) + 1e-06)
    clipped = factor * average
    new_momentum = 0.9 * outer_momentum + clipped
    new_global = (global_weights.astype(jnp.float32) - 0.7 * (clipped + 0.9 * new_momentum)).astype(jnp.bfloat16)
    alpha = 0.9 / (1.0 + 0.1 * outer_step.astype(jnp.float32))
    alpha = alpha[:, None, None]
    mixed_local = (alpha * local_weights.astype(jnp.float32) + (1.0 - alpha) * new_global.astype(jnp.float32)[None]).astype(jnp.bfloat16)
    return (new_global, new_momentum, mixed_local)
```

```python
import functools

import jax
import jax.numpy as jnp
from jax import lax
from jax.experimental import pallas as pl
from jax.experimental.pallas import tpu as pltpu
from jax.sharding import PartitionSpec as P

BLOCK = 128
SPLIT = 2.0**23 + 1.0


def one_bit(values):
    wide = values * SPLIT
    near = wide - (wide - values)
    return jnp.where(values >= 1.5 * near, near + near, near)


def quantize_kernel(global_ref, local_ref, decoded_ref):
    for start in range(0, global_ref.shape[1], BLOCK):
        lanes = pl.ds(start, BLOCK)
        delta = global_ref[:, lanes].astype(jnp.float32) - local_ref[:, lanes].astype(jnp.float32)
        magnitude = jnp.abs(delta)
        largest = jnp.maximum(jnp.max(magnitude, axis=1, keepdims=True), 2.0**-24)
        near = one_bit(largest)
        scale = jnp.minimum(jnp.where(near >= largest, near, near + near), 2.0**15)
        least = scale * 2.0**-7
        level = jnp.maximum(one_bit(magnitude), least + least)
        level = jnp.where(magnitude >= least, level, 0.0)
        decoded_ref[:, lanes] = jnp.where(delta < 0.0, -level, level).astype(jnp.bfloat16)


def quantize(global_weights, local_weights):
    rows, width = global_weights.shape
    tile = 16
    block = pl.BlockSpec((tile, width), lambda i: (i, 0))
    return pl.pallas_call(
        quantize_kernel,
        out_shape=jax.ShapeDtypeStruct((rows, width), jnp.bfloat16),
        grid=(rows // tile,),
        in_specs=[block, block],
        out_specs=block,
    )(global_weights, local_weights)


def exchange_sum(value, axis, groups, count):
    copies = jnp.broadcast_to(value[None], (count,) + value.shape)
    parts = lax.all_to_all(copies, axis, 0, 0, tiled=True, axis_index_groups=groups)
    return jnp.sum(parts, axis=0)


def total_over_devices(value, replicas, peers):
    value = exchange_sum(value, "rep", None, replicas)
    inner = 8
    outer = peers // inner
    near = [[i * inner + j for j in range(inner)] for i in range(outer)]
    far = [[i * inner + j for i in range(outer)] for j in range(inner)]
    value = exchange_sum(value, "fsdp", near, inner)
    return exchange_sum(value, "fsdp", far, outer)


def shards(global_weights, local_weights, outer_momentum, outer_step):
    replicas = lax.axis_size("rep")
    peers = lax.axis_size("fsdp")
    rows_dev, width = global_weights.shape
    share = rows_dev // replicas
    decoded = quantize(global_weights, local_weights[0])
    parts = lax.all_to_all(
        decoded.reshape(replicas, share, width), "rep", 0, 0, tiled=True
    )
    average = jnp.sum(parts.astype(jnp.float32), axis=0) / replicas
    partial = jnp.sum((average * average).reshape(share, width // BLOCK, BLOCK), axis=1)
    squares = jnp.sum(total_over_devices(partial, replicas, peers))
    entries = jnp.float32(rows_dev * peers * width)
    factor = 0.5 / jnp.sqrt(squares / entries + 1e-06)
    clipped = factor * average
    new_momentum = 0.9 * outer_momentum + clipped
    owned = lax.dynamic_slice_in_dim(global_weights, lax.axis_index("rep") * share, share, 0)
    new_share = (owned.astype(jnp.float32) - 0.7 * (clipped + 0.9 * new_momentum)).astype(
        jnp.bfloat16
    )
    new_global = lax.all_to_all(
        jnp.broadcast_to(new_share[None], (replicas, share, width)), "rep", 0, 0, tiled=True
    ).reshape(rows_dev, width)
    alpha = 0.9 / (1.0 + 0.1 * outer_step[0].astype(jnp.float32))
    mixed_local = (
        alpha * local_weights.astype(jnp.float32)
        + (1.0 - alpha) * new_global.astype(jnp.float32)[None]
    ).astype(jnp.bfloat16)
    return (new_global, new_momentum, mixed_local)


def solution(mesh):
    placed = (P("fsdp", None), P("rep", "fsdp", None), P(("fsdp", "rep"), None), P("rep"))
    return jax.shard_map(
        shards,
        mesh=mesh,
        in_specs=placed,
        out_specs=(P("fsdp", None), P(("fsdp", "rep"), None), P("rep", "fsdp", None)),
        check_vma=False,
    )
```

```python
import functools
import itertools

import jax
import jax.numpy as jnp
from jax import lax
from jax.experimental import pallas as pl
from jax.experimental.pallas import tpu as pltpu
from jax.sharding import PartitionSpec as P

BLOCK = 128
SPLIT = 2.0**23 + 1.0
VMEM = pltpu.CompilerParams(vmem_limit_bytes=24 * 2**20)
WHOLE = pl.BlockSpec(memory_space=pltpu.VMEM)


def one_bit(values):
    wide = values * SPLIT
    return wide - (wide - values)


def quantize_kernel(global_ref, local_ref, decoded_ref, global_tile, local_tile, decoded_tile, arrived, sent):
    step = 16
    count = global_ref.shape[0] // step

    def tile_rows(i):
        return pl.ds(pl.multiple_of(i * step, step), step)

    def fetch(i):
        return [
            pltpu.make_async_copy(ref.at[tile_rows(i)], tile.at[tile_rows(i)], arrived.at[k, i])
            for k, (ref, tile) in enumerate(((global_ref, global_tile), (local_ref, local_tile)))
        ]

    def put(i):
        return pltpu.make_async_copy(decoded_tile.at[tile_rows(i)], decoded_ref.at[tile_rows(i)], sent.at[i])

    for i in range(count):
        for copy in fetch(i):
            copy.start()

    @pl.loop(0, count)
    def _(i):
        for copy in fetch(i):
            copy.wait()
        for start in range(0, global_ref.shape[1], BLOCK):
            at = (tile_rows(i), pl.ds(start, BLOCK))
            delta = global_tile[at].astype(jnp.float32) - local_tile[at].astype(jnp.float32)
            magnitude = jnp.abs(delta)
            largest = jnp.maximum(jnp.max(magnitude, axis=1, keepdims=True), 2.0**-24)
            near = one_bit(largest)
            scale = jnp.minimum(jnp.where(near >= largest, near, near + near), 2.0**15)
            least = scale * 2.0**-7
            level = jnp.maximum(one_bit(magnitude), least + least)
            level = jnp.where(magnitude >= least, level, 0.0)
            decoded_tile[at] = jnp.where(delta < 0.0, -level, level).astype(jnp.bfloat16)
        put(i).start()

    for i in range(count):
        put(i).wait()


def quantize(global_weights, local_weights):
    shape = global_weights.shape
    far = pl.BlockSpec(memory_space=pl.ANY)
    steps = shape[0] // 16
    return pl.pallas_call(
        quantize_kernel,
        out_shape=jax.ShapeDtypeStruct(shape, jnp.bfloat16),
        in_specs=[far, far],
        out_specs=far,
        scratch_shapes=[
            pltpu.VMEM(shape, jnp.bfloat16),
            pltpu.VMEM(shape, jnp.bfloat16),
            pltpu.VMEM(shape, jnp.bfloat16),
            pltpu.SemaphoreType.DMA((2, steps)),
            pltpu.SemaphoreType.DMA((steps,)),
        ],
    )(global_weights, local_weights)


def total_kernel(parts_ref, momentum_ref, average_ref, carried_ref, squares_ref):
    squares = jnp.zeros((parts_ref.shape[1], BLOCK), jnp.float32)
    for start in range(0, parts_ref.shape[2], BLOCK):
        lanes = pl.ds(start, BLOCK)
        total = parts_ref[0, :, lanes].astype(jnp.float32)
        for r in range(1, parts_ref.shape[0]):
            total += parts_ref[r, :, lanes].astype(jnp.float32)
        average = total / parts_ref.shape[0]
        average_ref[:, lanes] = average
        squares += average * average
        momentum = momentum_ref[:, lanes]
        coarse = momentum.astype(jnp.bfloat16)
        carried_ref[0, :, lanes] = total.astype(jnp.bfloat16)
        carried_ref[1, :, lanes] = coarse
        carried_ref[2, :, lanes] = (momentum - coarse.astype(jnp.float32)).astype(jnp.bfloat16)
    for i in range(squares_ref.shape[0]):
        squares_ref[i] = squares


def totals(parts, momentum, copies):
    share, width = momentum.shape
    return pl.pallas_call(
        total_kernel,
        out_shape=(
            jax.ShapeDtypeStruct((share, width), jnp.float32),
            jax.ShapeDtypeStruct((3, share, width), jnp.bfloat16),
            jax.ShapeDtypeStruct((copies, share, BLOCK), jnp.float32),
        ),
        in_specs=[WHOLE, WHOLE],
        out_specs=(WHOLE, WHOLE, WHOLE),
        compiler_params=VMEM,
    )(parts, momentum)


def update_kernel(
    entries, replicas, layer_ref, step_ref, parts_ref, average_ref, momentum_ref, own_ref, behind_ref, ahead_ref,
    owned_ref, new_momentum_ref, copies_ref, alpha_ref,
):
    steps = jnp.full(alpha_ref.shape, step_ref[0], jnp.int32).astype(jnp.float32)
    alpha_ref[...] = 0.9 / (1.0 + 0.1 * steps)
    squares = jnp.sum(jnp.sum(parts_ref[...], axis=0), keepdims=True)
    factor = 0.5 / jnp.sqrt(squares / entries + 1e-06)
    part = factor / replicas
    layers = owned_ref.shape[0]
    step = 512
    for start in range(0, average_ref.shape[1], step):
        lanes = pl.ds(start, step)
        new_momentum_ref[:, lanes] = 0.9 * momentum_ref[:, lanes] + factor * average_ref[:, lanes]
    for away, carried_ref in enumerate((own_ref, behind_ref, ahead_ref)):
        layer = lax.rem(layer_ref[0] + layers - away, layers)
        for start in range(0, own_ref.shape[2], step):
            lanes = pl.ds(start, step)
            total, coarse, fine = (carried_ref[i, :, lanes].astype(jnp.float32) for i in range(3))
            clipped = part * total
            new_momentum = 0.9 * (coarse + fine) + clipped
            share = (
                owned_ref[layer, :, lanes].astype(jnp.float32) - 0.7 * (clipped + 0.9 * new_momentum)
            ).astype(jnp.bfloat16)
            for i in range(copies_ref.shape[0]):
                copies_ref[i, layer, :, lanes] = share


def update(entries, replicas, layer, outer_step, parts, average, momentum, own, behind, ahead, owned, copies):
    layers, share, width = owned.shape
    return pl.pallas_call(
        functools.partial(update_kernel, entries, replicas),
        out_shape=(
            jax.ShapeDtypeStruct((share, width), jnp.float32),
            jax.ShapeDtypeStruct((copies, layers, share, width), jnp.bfloat16),
            jax.ShapeDtypeStruct((share, BLOCK), jnp.float32),
        ),
        in_specs=[pl.BlockSpec(memory_space=pltpu.SMEM)] * 2 + [WHOLE] * 7,
        out_specs=(WHOLE, WHOLE, WHOLE),
        compiler_params=VMEM,
    )(layer, outer_step, parts, average, momentum, own, behind, ahead, owned)


def mix_kernel(alpha_ref, gathered_ref, local_ref, new_global_ref, mixed_ref):
    alpha = alpha_ref[:, 0:1]
    rest = 1.0 - alpha
    for i in range(gathered_ref.shape[0]):
        for start in range(0, gathered_ref.shape[3], 1024):
            lanes = pl.ds(start, 1024)
            new_global = gathered_ref[i, 0, :, lanes]
            new_global_ref[i, :, lanes] = new_global
            mixed_ref[i, :, lanes] = (
                alpha * local_ref[i, :, lanes].astype(jnp.float32) + rest * new_global.astype(jnp.float32)
            ).astype(jnp.bfloat16)


def mix(alpha, gathered, local_weights):
    columns, layers, share, width = gathered.shape
    block = pl.BlockSpec((columns, share, width), lambda i: (i, 0, 0))
    shape = jax.ShapeDtypeStruct((layers * columns, share, width), jnp.bfloat16)
    return pl.pallas_call(
        mix_kernel,
        out_shape=(shape, shape),
        grid=(layers,),
        in_specs=[WHOLE, pl.BlockSpec((columns, 1, share, width), lambda i: (0, i, 0, 0)), block],
        out_specs=(block, block),
        compiler_params=VMEM,
    )(alpha, gathered, local_weights.reshape(shape.shape))


def grouped(lengths, inside):
    names = list(lengths)
    strides = {n: 1 for n in names}
    for n, after in zip(names[-2::-1], names[:0:-1]):
        strides[n] = strides[after] * lengths[after]
    outside = [n for n in names if n not in inside]

    def offsets(axes):
        steps = [[i * strides[n] for i in range(lengths[n])] for n in axes]
        return [sum(each) for each in itertools.product(*steps)]

    return [[a + b for b in offsets(inside)] for a in offsets(outside)]


def exchange(copies, groups):
    return lax.all_to_all(copies, ("rep", "fsdp"), 0, 0, tiled=True, axis_index_groups=groups)


def shards(global_weights, local_weights, outer_momentum, outer_step):
    replicas = lax.axis_size("rep")
    peers = lax.axis_size("fsdp")
    rows_dev, width = global_weights.shape
    share = rows_dev // replicas
    lengths = dict(z_lo=3, x=4, y=8, z_hi=4, core=2)
    layers, columns = lengths["z_lo"], lengths["x"]
    place = lax.axis_index("rep")
    owned = lax.dynamic_index_in_dim(
        global_weights.reshape(layers, columns, share, width), lax.rem(place, columns), 1, keepdims=False
    )
    plane = grouped(lengths, ("x", "y"))
    line = grouped(lengths, ("z_lo", "z_hi", "core"))
    decoded = quantize(global_weights, local_weights[0])
    parts = lax.all_to_all(
        decoded.reshape(replicas, share, width), "rep", 0, 0, tiled=True
    )
    average, carried, partial = totals(parts, outer_momentum, len(line[0]))
    behind, ahead = (
        lax.ppermute(carried, "rep", [(i, (i + away * columns) % replicas) for i in range(replicas)])
        for away in (1, 2)
    )
    partial = jnp.sum(exchange(partial, line), axis=0)
    partials = exchange(jnp.broadcast_to(partial[None], (len(plane[0]),) + partial.shape), plane)
    entries = float(rows_dev * peers * width)
    layer = (place // columns).astype(jnp.int32)[None]
    new_momentum, copies, alpha = update(
        entries, replicas, layer, outer_step, partials, average, outer_momentum, carried, behind, ahead, owned, columns
    )
    beside = [[i * columns + j for j in range(columns)] for i in range(layers)]
    gathered = lax.all_to_all(copies, "rep", 0, 0, tiled=True, axis_index_groups=beside)
    new_global, mixed_local = mix(alpha, gathered, local_weights[0])
    return (
        new_global.reshape(rows_dev, width),
        new_momentum,
        mixed_local.reshape(local_weights.shape),
    )


def solution(mesh):
    placed = (P("fsdp", None), P("rep", "fsdp", None), P(("fsdp", "rep"), None), P("rep"))
    return jax.shard_map(
        shards,
        mesh=mesh,
        in_specs=placed,
        out_specs=(P("fsdp", None), P(("fsdp", "rep"), None), P("rep", "fsdp", None)),
        check_vma=False,
    )
```

```python
import functools
import itertools

import jax
import jax.numpy as jnp
from jax import lax
from jax.experimental import pallas as pl
from jax.experimental.pallas import tpu as pltpu
from jax.sharding import PartitionSpec as P

BLOCK = 128
SPLIT = 2.0**23 + 1.0
VMEM = pltpu.CompilerParams(vmem_limit_bytes=24 * 2**20)
WHOLE = pl.BlockSpec(memory_space=pltpu.VMEM)


def one_bit(values):
    wide = values * SPLIT
    return wide - (wide - values)


def quantize_kernel(global_ref, local_ref, decoded_ref, global_tile, local_tile, decoded_tile, arrived, sent):
    step = 16
    count = global_ref.shape[0] // step

    def tile_rows(i):
        return pl.ds(pl.multiple_of(i * step, step), step)

    def fetch(i):
        return [
            pltpu.make_async_copy(ref.at[tile_rows(i)], tile.at[tile_rows(i)], arrived.at[k, i])
            for k, (ref, tile) in enumerate(((global_ref, global_tile), (local_ref, local_tile)))
        ]

    def put(i):
        return pltpu.make_async_copy(decoded_tile.at[tile_rows(i)], decoded_ref.at[tile_rows(i)], sent.at[i])

    for i in range(count):
        for copy in fetch(i):
            copy.start()

    @pl.loop(0, count)
    def _(i):
        for copy in fetch(i):
            copy.wait()
        for start in range(0, global_ref.shape[1], BLOCK):
            at = (tile_rows(i), pl.ds(start, BLOCK))
            delta = global_tile[at].astype(jnp.float32) - local_tile[at].astype(jnp.float32)
            magnitude = jnp.abs(delta)
            largest = jnp.maximum(jnp.max(magnitude, axis=1, keepdims=True), 2.0**-24)
            near = one_bit(largest)
            scale = jnp.minimum(jnp.where(near >= largest, near, near + near), 2.0**15)
            least = scale * 2.0**-7
            level = jnp.maximum(one_bit(magnitude), least + least)
            level = jnp.where(magnitude >= least, level, 0.0)
            decoded_tile[at] = jnp.where(delta < 0.0, -level, level).astype(jnp.bfloat16)
        put(i).start()

    for i in range(count):
        put(i).wait()


def quantize(global_weights, local_weights):
    shape = global_weights.shape
    far = pl.BlockSpec(memory_space=pl.ANY)
    steps = shape[0] // 16
    return pl.pallas_call(
        quantize_kernel,
        out_shape=jax.ShapeDtypeStruct(shape, jnp.bfloat16),
        in_specs=[far, far],
        out_specs=far,
        scratch_shapes=[
            pltpu.VMEM(shape, jnp.bfloat16),
            pltpu.VMEM(shape, jnp.bfloat16),
            pltpu.VMEM(shape, jnp.bfloat16),
            pltpu.SemaphoreType.DMA((2, steps)),
            pltpu.SemaphoreType.DMA((steps,)),
        ],
    )(global_weights, local_weights)


def total_kernel(parts_ref, momentum_ref, average_ref, carried_ref, squares_ref):
    squares = jnp.zeros((parts_ref.shape[1], BLOCK), jnp.float32)
    for start in range(0, parts_ref.shape[2], BLOCK):
        lanes = pl.ds(start, BLOCK)
        total = parts_ref[0, :, lanes].astype(jnp.float32)
        for r in range(1, parts_ref.shape[0]):
            total += parts_ref[r, :, lanes].astype(jnp.float32)
        average = total / parts_ref.shape[0]
        average_ref[:, lanes] = average
        squares += average * average
        momentum = momentum_ref[:, lanes]
        coarse = momentum.astype(jnp.bfloat16)
        carried_ref[0, :, lanes] = total.astype(jnp.bfloat16)
        carried_ref[1, :, lanes] = coarse
        carried_ref[2, :, lanes] = (momentum - coarse.astype(jnp.float32)).astype(jnp.bfloat16)
    squares = jnp.sum(squares, axis=0, keepdims=True)
    for i in range(squares_ref.shape[0]):
        squares_ref[i] = squares


def totals(parts, momentum, copies):
    share, width = momentum.shape
    return pl.pallas_call(
        total_kernel,
        out_shape=(
            jax.ShapeDtypeStruct((share, width), jnp.float32),
            jax.ShapeDtypeStruct((3, share, width), jnp.bfloat16),
            jax.ShapeDtypeStruct((copies, 1, BLOCK), jnp.float32),
        ),
        in_specs=[WHOLE, WHOLE],
        out_specs=(WHOLE, WHOLE, WHOLE),
        compiler_params=VMEM,
    )(parts, momentum)


def update_kernel(
    entries, replicas, layer_ref, step_ref, parts_ref, average_ref, momentum_ref, own_ref, behind_ref, ahead_ref,
    owned_ref, new_momentum_ref, copies_ref, alpha_ref,
):
    steps = jnp.full(alpha_ref.shape, step_ref[0], jnp.int32).astype(jnp.float32)
    alpha_ref[...] = 0.9 / (1.0 + 0.1 * steps)
    squares = jnp.sum(jnp.sum(parts_ref[...], axis=0), keepdims=True)
    factor = 0.5 / jnp.sqrt(squares / entries + 1e-06)
    part = factor / replicas
    layers = owned_ref.shape[0]
    step = 512
    for start in range(0, average_ref.shape[1], step):
        lanes = pl.ds(start, step)
        new_momentum_ref[:, lanes] = 0.9 * momentum_ref[:, lanes] + factor * average_ref[:, lanes]
    for away, carried_ref in enumerate((own_ref, behind_ref, ahead_ref)):
        layer = lax.rem(layer_ref[0] + layers - away, layers)
        for start in range(0, own_ref.shape[2], step):
            lanes = pl.ds(start, step)
            total, coarse, fine = (carried_ref[i, :, lanes].astype(jnp.float32) for i in range(3))
            clipped = part * total
            new_momentum = 0.9 * (coarse + fine) + clipped
            share = (
                owned_ref[layer, :, lanes].astype(jnp.float32) - 0.7 * (clipped + 0.9 * new_momentum)
            ).astype(jnp.bfloat16)
            for i in range(copies_ref.shape[0]):
                copies_ref[i, layer, :, lanes] = share


def update(entries, replicas, layer, outer_step, parts, average, momentum, own, behind, ahead, owned, copies):
    layers, share, width = owned.shape
    return pl.pallas_call(
        functools.partial(update_kernel, entries, replicas),
        out_shape=(
            jax.ShapeDtypeStruct((share, width), jnp.float32),
            jax.ShapeDtypeStruct((copies, layers, share, width), jnp.bfloat16),
            jax.ShapeDtypeStruct((share, BLOCK), jnp.float32),
        ),
        in_specs=[pl.BlockSpec(memory_space=pltpu.SMEM)] * 2 + [WHOLE] * 7,
        out_specs=(WHOLE, WHOLE, WHOLE),
        compiler_params=VMEM,
    )(layer, outer_step, parts, average, momentum, own, behind, ahead, owned)


def mix_kernel(alpha_ref, gathered_ref, local_ref, new_global_ref, mixed_ref, mixed_tile, kept, sent):
    alpha = alpha_ref[:, 0:1]
    rest = 1.0 - alpha
    columns, layers, _, width = gathered_ref.shape
    copies = []
    for layer in range(layers):
        for i in range(columns):
            j = layer * columns + i
            copies.append(pltpu.make_async_copy(gathered_ref.at[i, layer], new_global_ref.at[j], kept.at[j]))
            copies[-1].start()
    for layer in range(layers):
        for i in range(columns):
            j = layer * columns + i
            for start in range(0, width, 1024):
                lanes = pl.ds(start, 1024)
                mixed_tile[j, :, lanes] = (
                    alpha * local_ref[j, :, lanes].astype(jnp.float32)
                    + rest * gathered_ref[i, layer, :, lanes].astype(jnp.float32)
                ).astype(jnp.bfloat16)
            copies.append(pltpu.make_async_copy(mixed_tile.at[j], mixed_ref.at[j], sent.at[j]))
            copies[-1].start()
    for copy in copies:
        copy.wait()


def mix(alpha, gathered, local_weights):
    columns, layers, share, width = gathered.shape
    count = layers * columns
    shape = jax.ShapeDtypeStruct((count, share, width), jnp.bfloat16)
    far = pl.BlockSpec(memory_space=pl.ANY)
    return pl.pallas_call(
        mix_kernel,
        out_shape=(shape, shape),
        in_specs=[WHOLE, WHOLE, WHOLE],
        out_specs=(far, far),
        scratch_shapes=[
            pltpu.VMEM(shape.shape, jnp.bfloat16),
            pltpu.SemaphoreType.DMA((count,)),
            pltpu.SemaphoreType.DMA((count,)),
        ],
        compiler_params=VMEM,
    )(alpha, gathered, local_weights.reshape(shape.shape))


def grouped(lengths, inside):
    names = list(lengths)
    strides = {n: 1 for n in names}
    for n, after in zip(names[-2::-1], names[:0:-1]):
        strides[n] = strides[after] * lengths[after]
    outside = [n for n in names if n not in inside]

    def offsets(axes):
        steps = [[i * strides[n] for i in range(lengths[n])] for n in axes]
        return [sum(each) for each in itertools.product(*steps)]

    return [[a + b for b in offsets(inside)] for a in offsets(outside)]


def exchange(copies, groups):
    return lax.all_to_all(copies, ("rep", "fsdp"), 0, 0, tiled=True, axis_index_groups=groups)


def shards(global_weights, local_weights, outer_momentum, outer_step):
    replicas = lax.axis_size("rep")
    peers = lax.axis_size("fsdp")
    rows_dev, width = global_weights.shape
    share = rows_dev // replicas
    lengths = dict(z_lo=3, x=4, y=8, z_hi=4, core=2)
    layers, columns = lengths["z_lo"], lengths["x"]
    place = lax.axis_index("rep")
    owned = lax.dynamic_index_in_dim(
        global_weights.reshape(layers, columns, share, width), lax.rem(place, columns), 1, keepdims=False
    )
    plane = grouped(lengths, ("x", "y"))
    line = grouped(lengths, ("z_lo", "z_hi", "core"))
    decoded = quantize(global_weights, local_weights[0])
    parts = lax.all_to_all(
        decoded.reshape(replicas, share, width), "rep", 0, 0, tiled=True
    )
    average, carried, partial = totals(parts, outer_momentum, len(line[0]))
    behind, ahead = (
        lax.ppermute(carried, "rep", [(i, (i + away * columns) % replicas) for i in range(replicas)])
        for away in (1, 2)
    )
    partial = jnp.sum(exchange(partial, line), axis=0)
    partials = exchange(jnp.broadcast_to(partial[None], (len(plane[0]),) + partial.shape), plane)
    entries = float(rows_dev * peers * width)
    layer = (place // columns).astype(jnp.int32)[None]
    new_momentum, copies, alpha = update(
        entries, replicas, layer, outer_step, partials, average, outer_momentum, carried, behind, ahead, owned, columns
    )
    beside = [[i * columns + j for j in range(columns)] for i in range(layers)]
    gathered = lax.all_to_all(copies, "rep", 0, 0, tiled=True, axis_index_groups=beside)
    new_global, mixed_local = mix(alpha, gathered, local_weights[0])
    return (
        new_global.reshape(rows_dev, width),
        new_momentum,
        mixed_local.reshape(local_weights.shape),
    )


def solution(mesh):
    placed = (P("fsdp", None), P("rep", "fsdp", None), P(("fsdp", "rep"), None), P("rep"))
    return jax.shard_map(
        shards,
        mesh=mesh,
        in_specs=placed,
        out_specs=(P("fsdp", None), P(("fsdp", "rep"), None), P("rep", "fsdp", None)),
        check_vma=False,
    )
```

```python
import functools
import itertools

import jax
import jax.numpy as jnp
from jax import lax
from jax.experimental import pallas as pl
from jax.experimental.pallas import tpu as pltpu
from jax.sharding import PartitionSpec as P

BLOCK = 128
SPLIT = 2.0**23 + 1.0
VMEM = pltpu.CompilerParams(vmem_limit_bytes=24 * 2**20)
WHOLE = pl.BlockSpec(memory_space=pltpu.VMEM)


def one_bit(values):
    wide = values * SPLIT
    return wide - (wide - values)


def quantize_kernel(global_ref, local_ref, decoded_ref, global_tile, local_tile, decoded_tile, arrived, sent):
    step = 16
    count = global_ref.shape[0] // step

    def tile_rows(i):
        return pl.ds(pl.multiple_of(i * step, step), step)

    def fetch(i):
        return [
            pltpu.make_async_copy(ref.at[tile_rows(i)], tile.at[tile_rows(i)], arrived.at[k, i])
            for k, (ref, tile) in enumerate(((global_ref, global_tile), (local_ref, local_tile)))
        ]

    def put(i):
        slot = lax.rem(4 * (i // 2) + 3 * lax.rem(i, 2), 6)
        return pltpu.make_async_copy(decoded_tile.at[tile_rows(i)], decoded_ref.at[tile_rows(slot)], sent.at[i])

    for i in range(count):
        for copy in fetch(i):
            copy.start()

    @pl.loop(0, count)
    def _(i):
        for copy in fetch(i):
            copy.wait()
        for start in range(0, global_ref.shape[1], BLOCK):
            at = (tile_rows(i), pl.ds(start, BLOCK))
            delta = global_tile[at].astype(jnp.float32) - local_tile[at].astype(jnp.float32)
            magnitude = jnp.abs(delta)
            largest = jnp.maximum(jnp.max(magnitude, axis=1, keepdims=True), 2.0**-24)
            near = one_bit(largest)
            scale = jnp.minimum(jnp.where(near >= largest, near, near + near), 2.0**15)
            least = scale * 2.0**-7
            level = jnp.maximum(one_bit(magnitude), least + least)
            level = jnp.where(magnitude >= least, level, 0.0)
            decoded_tile[at] = jnp.where(delta < 0.0, -level, level).astype(jnp.bfloat16)
        put(i).start()

    for i in range(count):
        put(i).wait()


def quantize(global_weights, local_weights):
    shape = global_weights.shape
    far = pl.BlockSpec(memory_space=pl.ANY)
    steps = shape[0] // 16
    return pl.pallas_call(
        quantize_kernel,
        out_shape=jax.ShapeDtypeStruct(shape, jnp.bfloat16),
        in_specs=[far, far],
        out_specs=far,
        scratch_shapes=[
            pltpu.VMEM(shape, jnp.bfloat16),
            pltpu.VMEM(shape, jnp.bfloat16),
            pltpu.VMEM(shape, jnp.bfloat16),
            pltpu.SemaphoreType.DMA((2, steps)),
            pltpu.SemaphoreType.DMA((steps,)),
        ],
    )(global_weights, local_weights)


def total_kernel(parts_ref, momentum_ref, average_ref, carried_ref, squares_ref):
    squares = jnp.zeros((parts_ref.shape[1], BLOCK), jnp.float32)
    for start in range(0, parts_ref.shape[2], BLOCK):
        lanes = pl.ds(start, BLOCK)
        total = parts_ref[0, :, lanes].astype(jnp.float32)
        for r in range(1, parts_ref.shape[0]):
            total += parts_ref[r, :, lanes].astype(jnp.float32)
        average = total / parts_ref.shape[0]
        average_ref[:, lanes] = average
        squares += average * average
        momentum = momentum_ref[:, lanes]
        coarse = momentum.astype(jnp.bfloat16)
        carried_ref[0, :, lanes] = total.astype(jnp.bfloat16)
        carried_ref[1, :, lanes] = coarse
        carried_ref[2, :, lanes] = (momentum - coarse.astype(jnp.float32)).astype(jnp.bfloat16)
    squares = jnp.sum(squares, axis=0, keepdims=True)
    for i in range(squares_ref.shape[0]):
        squares_ref[i] = squares


def totals(parts, momentum, copies):
    share, width = momentum.shape
    return pl.pallas_call(
        total_kernel,
        out_shape=(
            jax.ShapeDtypeStruct((share, width), jnp.float32),
            jax.ShapeDtypeStruct((3, share, width), jnp.bfloat16),
            jax.ShapeDtypeStruct((copies, 1, BLOCK), jnp.float32),
        ),
        in_specs=[WHOLE, WHOLE],
        out_specs=(WHOLE, WHOLE, WHOLE),
        compiler_params=VMEM,
    )(parts, momentum)


def update_kernel(
    entries, replicas, layer_ref, step_ref, parts_ref, own_ref, behind_ref, ahead_ref, owned_ref,
    copies_ref, alpha_ref, factor_ref,
):
    steps = jnp.full(alpha_ref.shape, step_ref[0], jnp.int32).astype(jnp.float32)
    alpha_ref[...] = 0.9 / (1.0 + 0.1 * steps)
    squares = jnp.sum(jnp.sum(parts_ref[...], axis=0), keepdims=True)
    factor = 0.5 / jnp.sqrt(squares / entries + 1e-06)
    part = factor / replicas
    factor_ref[...] = jnp.broadcast_to(factor, factor_ref.shape)
    layers = owned_ref.shape[0]
    step = 512
    for away, carried_ref in enumerate((own_ref, behind_ref, ahead_ref)):
        layer = lax.rem(layer_ref[0] + layers - away, layers)
        for start in range(0, own_ref.shape[2], step):
            lanes = pl.ds(start, step)
            total, coarse, fine = (carried_ref[i, :, lanes].astype(jnp.float32) for i in range(3))
            clipped = part * total
            new_momentum = 0.9 * (coarse + fine) + clipped
            share = (
                owned_ref[layer, :, lanes].astype(jnp.float32) - 0.7 * (clipped + 0.9 * new_momentum)
            ).astype(jnp.bfloat16)
            for i in range(copies_ref.shape[0]):
                copies_ref[i, layer, :, lanes] = share


def update(entries, replicas, layer, outer_step, parts, own, behind, ahead, owned, copies):
    layers, share, width = owned.shape
    tile = jax.ShapeDtypeStruct((share, BLOCK), jnp.float32)
    return pl.pallas_call(
        functools.partial(update_kernel, entries, replicas),
        out_shape=(jax.ShapeDtypeStruct((copies, layers, share, width), jnp.bfloat16), tile, tile),
        in_specs=[pl.BlockSpec(memory_space=pltpu.SMEM)] * 2 + [WHOLE] * 5,
        out_specs=(WHOLE,) * 3,
        compiler_params=VMEM,
    )(layer, outer_step, parts, own, behind, ahead, owned)


def mix_kernel(
    order, alpha_ref, factor_ref, average_ref, momentum_ref, gathered_ref, local_ref,
    new_global_ref, new_momentum_ref, mixed_ref, momentum_tile, mixed_tile, stored, kept, sent,
):
    alpha = alpha_ref[:, 0:1]
    rest = 1.0 - alpha
    factor = factor_ref[:, 0:1]
    columns, layers, _, width = gathered_ref.shape
    copies = []
    for layer in range(layers):
        for i, column in enumerate(order):
            j = layer * columns + column
            copies.append(pltpu.make_async_copy(gathered_ref.at[i, layer], new_global_ref.at[j], kept.at[j]))
            copies[-1].start()
    for start in range(0, width, 1024):
        lanes = pl.ds(start, 1024)
        momentum_tile[:, lanes] = 0.9 * momentum_ref[:, lanes] + factor * average_ref[:, lanes]
    copies.append(pltpu.make_async_copy(momentum_tile, new_momentum_ref, stored))
    copies[-1].start()
    for layer in range(layers):
        for i, column in enumerate(order):
            j = layer * columns + column
            for start in range(0, width, 1024):
                lanes = pl.ds(start, 1024)
                mixed_tile[j, :, lanes] = (
                    alpha * local_ref[j, :, lanes].astype(jnp.float32)
                    + rest * gathered_ref[i, layer, :, lanes].astype(jnp.float32)
                ).astype(jnp.bfloat16)
            copies.append(pltpu.make_async_copy(mixed_tile.at[j], mixed_ref.at[j], sent.at[j]))
            copies[-1].start()
    for copy in copies:
        copy.wait()


def mix(order, alpha, factor, average, momentum, gathered, local_weights):
    columns, layers, share, width = gathered.shape
    count = layers * columns
    shape = jax.ShapeDtypeStruct((count, share, width), jnp.bfloat16)
    far = pl.BlockSpec(memory_space=pl.ANY)
    return pl.pallas_call(
        functools.partial(mix_kernel, order),
        out_shape=(shape, jax.ShapeDtypeStruct(momentum.shape, jnp.float32), shape),
        in_specs=[WHOLE] * 6,
        out_specs=(far,) * 3,
        scratch_shapes=[
            pltpu.VMEM(momentum.shape, jnp.float32),
            pltpu.VMEM(shape.shape, jnp.bfloat16),
            pltpu.SemaphoreType.DMA(()),
            pltpu.SemaphoreType.DMA((count,)),
            pltpu.SemaphoreType.DMA((count,)),
        ],
        compiler_params=VMEM,
    )(alpha, factor, average, momentum, gathered, local_weights.reshape(shape.shape))


def grouped(lengths, inside):
    names = list(lengths)
    strides = {n: 1 for n in names}
    for n, after in zip(names[-2::-1], names[:0:-1]):
        strides[n] = strides[after] * lengths[after]
    outside = [n for n in names if n not in inside]

    def offsets(axes):
        steps = [[i * strides[n] for i in range(lengths[n])] for n in axes]
        return [sum(each) for each in itertools.product(*steps)]

    return [[a + b for b in offsets(inside)] for a in offsets(outside)]


def exchange(copies, groups):
    return lax.all_to_all(copies, ("rep", "fsdp"), 0, 0, tiled=True, axis_index_groups=groups)


def shards(global_weights, local_weights, outer_momentum, outer_step):
    replicas = lax.axis_size("rep")
    peers = lax.axis_size("fsdp")
    rows_dev, width = global_weights.shape
    share = rows_dev // replicas
    lengths = dict(z_lo=3, x=4, y=8, z_hi=4, core=2)
    layers, columns = lengths["z_lo"], lengths["x"]
    place = lax.axis_index("rep")
    owned = lax.dynamic_index_in_dim(
        global_weights.reshape(layers, columns, share, width), lax.rem(place, columns), 1, keepdims=False
    )
    plane = grouped(lengths, ("x", "y"))
    line = grouped(lengths, ("z_lo", "z_hi", "core"))
    decoded = quantize(global_weights, local_weights[0])
    slots = [(s % 3) * columns + (s % 2) * 2 + i for s in range(replicas // 2) for i in range(2)]
    parts = lax.all_to_all(
        decoded.reshape(replicas, share, width), "rep", 0, 0, tiled=True, axis_index_groups=[slots]
    )
    average, carried, partial = totals(parts, outer_momentum, len(line[0]))
    behind, ahead = (
        lax.ppermute(carried, "rep", [(i, (i + away * columns) % replicas) for i in range(replicas)])
        for away in (1, 2)
    )
    partial = jnp.sum(exchange(partial, line), axis=0)
    partials = exchange(jnp.broadcast_to(partial[None], (len(plane[0]),) + partial.shape), plane)
    entries = float(rows_dev * peers * width)
    layer = (place // columns).astype(jnp.int32)[None]
    copies, alpha, factor = update(
        entries, replicas, layer, outer_step, partials, carried, behind, ahead, owned, columns
    )
    order = (0, 1, 3, 2)
    beside = [[i * columns + j for j in order] for i in range(layers)]
    gathered = lax.all_to_all(copies, "rep", 0, 0, tiled=True, axis_index_groups=beside)
    new_global, new_momentum, mixed_local = mix(
        order, alpha, factor, average, outer_momentum, gathered, local_weights[0]
    )
    return (
        new_global.reshape(rows_dev, width),
        new_momentum,
        mixed_local.reshape(local_weights.shape),
    )


def solution(mesh):
    placed = (P("fsdp", None), P("rep", "fsdp", None), P(("fsdp", "rep"), None), P("rep"))
    return jax.shard_map(
        shards,
        mesh=mesh,
        in_specs=placed,
        out_specs=(P("fsdp", None), P(("fsdp", "rep"), None), P("rep", "fsdp", None)),
        check_vma=False,
    )
```

```python
import functools
import itertools

import jax
import jax.numpy as jnp
from jax import lax
from jax.experimental import pallas as pl
from jax.experimental.pallas import tpu as pltpu
from jax.sharding import PartitionSpec as P

BLOCK = 128
SPLIT = 2.0**23 + 1.0
TILES = (3, 5, 2, 0, 4, 1)
VMEM = pltpu.CompilerParams(vmem_limit_bytes=24 * 2**20)
WHOLE = pl.BlockSpec(memory_space=pltpu.VMEM)


def one_bit(values):
    wide = values * SPLIT
    return wide - (wide - values)


def quantize_kernel(global_ref, local_ref, decoded_ref, global_tile, local_tile, decoded_tile, arrived, sent):
    step = 16
    count = global_ref.shape[0] // step

    def tile_rows(i):
        return pl.ds(pl.multiple_of(i * step, step), step)

    def fetch(i):
        return [
            pltpu.make_async_copy(ref.at[tile_rows(i)], tile.at[tile_rows(i)], arrived.at[k, i])
            for k, (ref, tile) in enumerate(((global_ref, global_tile), (local_ref, local_tile)))
        ]

    def put(i):
        slot = sum(jnp.where(i == tile, s, 0) for s, tile in enumerate(TILES))
        return pltpu.make_async_copy(decoded_tile.at[tile_rows(i)], decoded_ref.at[tile_rows(slot)], sent.at[i])

    for i in range(count):
        for copy in fetch(i):
            copy.start()

    @pl.loop(0, count)
    def _(i):
        for copy in fetch(i):
            copy.wait()
        for start in range(0, global_ref.shape[1], BLOCK):
            at = (tile_rows(i), pl.ds(start, BLOCK))
            delta = global_tile[at].astype(jnp.float32) - local_tile[at].astype(jnp.float32)
            magnitude = jnp.abs(delta)
            largest = jnp.maximum(jnp.max(magnitude, axis=1, keepdims=True), 2.0**-24)
            scale = jnp.minimum(one_bit(largest * (1.5 - 2.0**-23)), 2.0**15)
            least = scale * 2.0**-7
            level = jnp.maximum(one_bit(magnitude), least + least)
            level = jnp.where(magnitude >= least, level, 0.0)
            decoded_tile[at] = jnp.where(delta < 0.0, -level, level).astype(jnp.bfloat16)
        put(i).start()

    for i in range(count):
        put(i).wait()


def quantize(global_weights, local_weights):
    shape = global_weights.shape
    far = pl.BlockSpec(memory_space=pl.ANY)
    steps = shape[0] // 16
    return pl.pallas_call(
        quantize_kernel,
        out_shape=jax.ShapeDtypeStruct(shape, jnp.bfloat16),
        in_specs=[far, far],
        out_specs=far,
        scratch_shapes=[
            pltpu.VMEM(shape, jnp.bfloat16),
            pltpu.VMEM(shape, jnp.bfloat16),
            pltpu.VMEM(shape, jnp.bfloat16),
            pltpu.SemaphoreType.DMA((2, steps)),
            pltpu.SemaphoreType.DMA((steps,)),
        ],
    )(global_weights, local_weights)


def total_kernel(parts_ref, momentum_ref, average_ref, carried_ref, squares_ref):
    squares = jnp.zeros((parts_ref.shape[1], BLOCK), jnp.float32)
    for start in range(0, parts_ref.shape[2], BLOCK):
        lanes = pl.ds(start, BLOCK)
        total = parts_ref[0, :, lanes].astype(jnp.float32)
        for r in range(1, parts_ref.shape[0]):
            total += parts_ref[r, :, lanes].astype(jnp.float32)
        average = total / parts_ref.shape[0]
        average_ref[:, lanes] = average
        squares += average * average
        momentum = momentum_ref[:, lanes]
        coarse = momentum.astype(jnp.bfloat16)
        carried_ref[0, :, lanes] = total.astype(jnp.bfloat16)
        carried_ref[1, :, lanes] = coarse
        carried_ref[2, :, lanes] = (momentum - coarse.astype(jnp.float32)).astype(jnp.bfloat16)
    squares = jnp.sum(squares, axis=0, keepdims=True)
    for i in range(squares_ref.shape[0]):
        squares_ref[i] = squares


def totals(parts, momentum, copies):
    share, width = momentum.shape
    return pl.pallas_call(
        total_kernel,
        out_shape=(
            jax.ShapeDtypeStruct((share, width), jnp.float32),
            jax.ShapeDtypeStruct((3, share, width), jnp.bfloat16),
            jax.ShapeDtypeStruct((copies, 1, BLOCK), jnp.float32),
        ),
        in_specs=[WHOLE, WHOLE],
        out_specs=(WHOLE, WHOLE, WHOLE),
        compiler_params=VMEM,
    )(parts, momentum)


def update_kernel(
    entries, replicas, layer_ref, step_ref, parts_ref, own_ref, behind_ref, ahead_ref, owned_ref,
    copies_ref, alpha_ref, factor_ref,
):
    steps = jnp.full(alpha_ref.shape, step_ref[0], jnp.int32).astype(jnp.float32)
    alpha_ref[...] = 0.9 / (1.0 + 0.1 * steps)
    squares = jnp.sum(jnp.sum(parts_ref[...], axis=0), keepdims=True)
    factor = 0.5 / jnp.sqrt(squares / entries + 1e-06)
    part = factor / replicas
    factor_ref[...] = jnp.broadcast_to(factor, factor_ref.shape)
    layers = owned_ref.shape[0]
    step = 512
    for away, carried_ref in enumerate((own_ref, behind_ref, ahead_ref)):
        layer = lax.rem(layer_ref[0] + layers - away, layers)
        for start in range(0, own_ref.shape[2], step):
            lanes = pl.ds(start, step)
            total, coarse, fine = (carried_ref[i, :, lanes].astype(jnp.float32) for i in range(3))
            clipped = part * total
            new_momentum = 0.9 * (coarse + fine) + clipped
            share = (
                owned_ref[layer, :, lanes].astype(jnp.float32) - 0.7 * (clipped + 0.9 * new_momentum)
            ).astype(jnp.bfloat16)
            for i in range(copies_ref.shape[0]):
                copies_ref[i, layer, :, lanes] = share


def update(entries, replicas, layer, outer_step, parts, own, behind, ahead, owned, copies):
    layers, share, width = owned.shape
    tile = jax.ShapeDtypeStruct((share, BLOCK), jnp.float32)
    return pl.pallas_call(
        functools.partial(update_kernel, entries, replicas),
        out_shape=(jax.ShapeDtypeStruct((copies, layers, share, width), jnp.bfloat16), tile, tile),
        in_specs=[pl.BlockSpec(memory_space=pltpu.SMEM)] * 2 + [WHOLE] * 5,
        out_specs=(WHOLE,) * 3,
        compiler_params=VMEM,
    )(layer, outer_step, parts, own, behind, ahead, owned)


def mix_kernel(
    order, alpha_ref, factor_ref, average_ref, momentum_ref, gathered_ref, local_ref,
    new_global_ref, new_momentum_ref, mixed_ref, momentum_tile, mixed_tile, stored, kept, sent,
):
    alpha = alpha_ref[:, 0:1]
    rest = 1.0 - alpha
    factor = factor_ref[:, 0:1]
    columns, layers, _, width = gathered_ref.shape
    copies = []
    for layer in range(layers):
        for i, column in enumerate(order):
            j = layer * columns + column
            copies.append(pltpu.make_async_copy(gathered_ref.at[i, layer], new_global_ref.at[j], kept.at[j]))
            copies[-1].start()
    for start in range(0, width, 1024):
        lanes = pl.ds(start, 1024)
        momentum_tile[:, lanes] = 0.9 * momentum_ref[:, lanes] + factor * average_ref[:, lanes]
    copies.append(pltpu.make_async_copy(momentum_tile, new_momentum_ref, stored))
    copies[-1].start()
    for layer in range(layers):
        for i, column in enumerate(order):
            j = layer * columns + column
            for start in range(0, width, 1024):
                lanes = pl.ds(start, 1024)
                mixed_tile[j, :, lanes] = (
                    alpha * local_ref[j, :, lanes].astype(jnp.float32)
                    + rest * gathered_ref[i, layer, :, lanes].astype(jnp.float32)
                ).astype(jnp.bfloat16)
            copies.append(pltpu.make_async_copy(mixed_tile.at[j], mixed_ref.at[j], sent.at[j]))
            copies[-1].start()
    for copy in copies:
        copy.wait()


def mix(order, alpha, factor, average, momentum, gathered, local_weights):
    columns, layers, share, width = gathered.shape
    count = layers * columns
    shape = jax.ShapeDtypeStruct((count, share, width), jnp.bfloat16)
    far = pl.BlockSpec(memory_space=pl.ANY)
    return pl.pallas_call(
        functools.partial(mix_kernel, order),
        out_shape=(shape, jax.ShapeDtypeStruct(momentum.shape, jnp.float32), shape),
        in_specs=[WHOLE] * 6,
        out_specs=(far,) * 3,
        scratch_shapes=[
            pltpu.VMEM(momentum.shape, jnp.float32),
            pltpu.VMEM(shape.shape, jnp.bfloat16),
            pltpu.SemaphoreType.DMA(()),
            pltpu.SemaphoreType.DMA((count,)),
            pltpu.SemaphoreType.DMA((count,)),
        ],
        compiler_params=VMEM,
    )(alpha, factor, average, momentum, gathered, local_weights.reshape(shape.shape))


def grouped(lengths, inside):
    names = list(lengths)
    strides = {n: 1 for n in names}
    for n, after in zip(names[-2::-1], names[:0:-1]):
        strides[n] = strides[after] * lengths[after]
    outside = [n for n in names if n not in inside]

    def offsets(axes):
        steps = [[i * strides[n] for i in range(lengths[n])] for n in axes]
        return [sum(each) for each in itertools.product(*steps)]

    return [[a + b for b in offsets(inside)] for a in offsets(outside)]


def exchange(copies, groups):
    return lax.all_to_all(copies, ("rep", "fsdp"), 0, 0, tiled=True, axis_index_groups=groups)


def shards(global_weights, local_weights, outer_momentum, outer_step):
    replicas = lax.axis_size("rep")
    peers = lax.axis_size("fsdp")
    rows_dev, width = global_weights.shape
    share = rows_dev // replicas
    lengths = dict(z_lo=3, x=4, y=8, z_hi=4, core=2)
    layers, columns = lengths["z_lo"], lengths["x"]
    place = lax.axis_index("rep")
    owned = lax.dynamic_index_in_dim(
        global_weights.reshape(layers, columns, share, width), lax.rem(place, columns), 1, keepdims=False
    )
    plane = grouped(lengths, ("x", "y"))
    line = grouped(lengths, ("z_lo", "z_hi", "core"))
    decoded = quantize(global_weights, local_weights[0])
    slots = [2 * tile + i for tile in TILES for i in range(2)]
    parts = lax.all_to_all(
        decoded.reshape(replicas, share, width), "rep", 0, 0, tiled=True, axis_index_groups=[slots]
    )
    average, carried, partial = totals(parts, outer_momentum, len(line[0]))
    behind, ahead = (
        lax.ppermute(carried, "rep", [(i, (i + away * columns) % replicas) for i in range(replicas)])
        for away in (1, 2)
    )
    partial = jnp.sum(exchange(partial, line), axis=0)
    partials = exchange(jnp.broadcast_to(partial[None], (len(plane[0]),) + partial.shape), plane)
    entries = float(rows_dev * peers * width)
    layer = (place // columns).astype(jnp.int32)[None]
    copies, alpha, factor = update(
        entries, replicas, layer, outer_step, partials, carried, behind, ahead, owned, columns
    )
    order = (0, 1, 3, 2)
    beside = [[i * columns + j for j in order] for i in range(layers)]
    gathered = lax.all_to_all(copies, "rep", 0, 0, tiled=True, axis_index_groups=beside)
    new_global, new_momentum, mixed_local = mix(
        order, alpha, factor, average, outer_momentum, gathered, local_weights[0]
    )
    return (
        new_global.reshape(rows_dev, width),
        new_momentum,
        mixed_local.reshape(local_weights.shape),
    )


def solution(mesh):
    placed = (P("fsdp", None), P("rep", "fsdp", None), P(("fsdp", "rep"), None), P("rep"))
    return jax.shard_map(
        shards,
        mesh=mesh,
        in_specs=placed,
        out_specs=(P("fsdp", None), P(("fsdp", "rep"), None), P("rep", "fsdp", None)),
        check_vma=False,
    )
```

```python
import functools
import itertools

import jax
import jax.numpy as jnp
from jax import lax
from jax.experimental import pallas as pl
from jax.experimental.pallas import tpu as pltpu
from jax.sharding import PartitionSpec as P

BLOCK = 128
SPLIT = 2.0**23 + 1.0
TILES = (2, 0, 5, 4, 1, 3)
VMEM = pltpu.CompilerParams(vmem_limit_bytes=24 * 2**20)
WHOLE = pl.BlockSpec(memory_space=pltpu.VMEM)


def one_bit(values):
    wide = values * SPLIT
    return wide - (wide - values)


def quantize_kernel(global_ref, local_ref, decoded_ref, global_tile, local_tile, decoded_tile, arrived, sent):
    step = 16
    count = global_ref.shape[0] // step

    def tile_rows(i):
        return pl.ds(pl.multiple_of(i * step, step), step)

    def fetch(i):
        return [
            pltpu.make_async_copy(ref.at[tile_rows(i)], tile.at[tile_rows(i)], arrived.at[k, i])
            for k, (ref, tile) in enumerate(((global_ref, global_tile), (local_ref, local_tile)))
        ]

    def put(i):
        slot = sum(jnp.where(i == tile, s, 0) for s, tile in enumerate(TILES))
        return pltpu.make_async_copy(decoded_tile.at[tile_rows(i)], decoded_ref.at[tile_rows(slot)], sent.at[i])

    for i in range(count):
        for copy in fetch(i):
            copy.start()

    @pl.loop(0, count)
    def _(i):
        for copy in fetch(i):
            copy.wait()
        for start in range(0, global_ref.shape[1], BLOCK):
            at = (tile_rows(i), pl.ds(start, BLOCK))
            delta = global_tile[at].astype(jnp.float32) - local_tile[at].astype(jnp.float32)
            magnitude = jnp.abs(delta)
            largest = jnp.maximum(jnp.max(magnitude, axis=1, keepdims=True), 2.0**-24)
            scale = jnp.minimum(one_bit(largest * (1.5 - 2.0**-23)), 2.0**15)
            least = scale * 2.0**-7
            level = jnp.maximum(one_bit(magnitude), least + least)
            level = jnp.where(magnitude >= least, level, 0.0)
            decoded_tile[at] = jnp.where(delta < 0.0, -level, level).astype(jnp.bfloat16)
        put(i).start()

    for i in range(count):
        put(i).wait()


def quantize(global_weights, local_weights):
    shape = global_weights.shape
    far = pl.BlockSpec(memory_space=pl.ANY)
    steps = shape[0] // 16
    return pl.pallas_call(
        quantize_kernel,
        out_shape=jax.ShapeDtypeStruct(shape, jnp.bfloat16),
        in_specs=[far, far],
        out_specs=far,
        scratch_shapes=[
            pltpu.VMEM(shape, jnp.bfloat16),
            pltpu.VMEM(shape, jnp.bfloat16),
            pltpu.VMEM(shape, jnp.bfloat16),
            pltpu.SemaphoreType.DMA((2, steps)),
            pltpu.SemaphoreType.DMA((steps,)),
        ],
    )(global_weights, local_weights)


def total_kernel(parts_ref, momentum_ref, average_ref, carried_ref, squares_ref):
    squares = jnp.zeros((parts_ref.shape[1], BLOCK), jnp.float32)
    for start in range(0, parts_ref.shape[2], BLOCK):
        lanes = pl.ds(start, BLOCK)
        total = parts_ref[0, :, lanes].astype(jnp.float32)
        for r in range(1, parts_ref.shape[0]):
            total += parts_ref[r, :, lanes].astype(jnp.float32)
        average = total / parts_ref.shape[0]
        average_ref[:, lanes] = average
        squares += average * average
        momentum = momentum_ref[:, lanes]
        coarse = momentum.astype(jnp.bfloat16)
        carried_ref[0, :, lanes] = total.astype(jnp.bfloat16)
        carried_ref[1, :, lanes] = coarse
        carried_ref[2, :, lanes] = (momentum - coarse.astype(jnp.float32)).astype(jnp.bfloat16)
    squares = jnp.sum(squares, axis=0, keepdims=True)
    for i in range(squares_ref.shape[0]):
        squares_ref[i] = squares


def totals(parts, momentum, copies):
    share, width = momentum.shape
    return pl.pallas_call(
        total_kernel,
        out_shape=(
            jax.ShapeDtypeStruct((share, width), jnp.float32),
            jax.ShapeDtypeStruct((3, share, width), jnp.bfloat16),
            jax.ShapeDtypeStruct((copies, 1, BLOCK), jnp.float32),
        ),
        in_specs=[WHOLE, WHOLE],
        out_specs=(WHOLE, WHOLE, WHOLE),
        compiler_params=VMEM,
    )(parts, momentum)


def update_kernel(
    entries, replicas, layer_ref, step_ref, parts_ref, own_ref, behind_ref, ahead_ref, owned_ref,
    copies_ref, alpha_ref, factor_ref,
):
    steps = jnp.full(alpha_ref.shape, step_ref[0], jnp.int32).astype(jnp.float32)
    alpha_ref[...] = 0.9 / (1.0 + 0.1 * steps)
    squares = jnp.sum(jnp.sum(parts_ref[...], axis=0), keepdims=True)
    factor = 0.5 / jnp.sqrt(squares / entries + 1e-06)
    part = factor / replicas
    factor_ref[...] = jnp.broadcast_to(factor, factor_ref.shape)
    layers = owned_ref.shape[0]
    step = 512
    for away, carried_ref in enumerate((own_ref, behind_ref, ahead_ref)):
        layer = lax.rem(layer_ref[0] + layers - away, layers)
        for start in range(0, own_ref.shape[2], step):
            lanes = pl.ds(start, step)
            total, coarse, fine = (carried_ref[i, :, lanes].astype(jnp.float32) for i in range(3))
            clipped = part * total
            new_momentum = 0.9 * (coarse + fine) + clipped
            share = (
                owned_ref[layer, :, lanes].astype(jnp.float32) - 0.7 * (clipped + 0.9 * new_momentum)
            ).astype(jnp.bfloat16)
            for i in range(copies_ref.shape[0]):
                copies_ref[i, layer, :, lanes] = share


def update(entries, replicas, layer, outer_step, parts, own, behind, ahead, owned, copies):
    layers, share, width = owned.shape
    tile = jax.ShapeDtypeStruct((share, BLOCK), jnp.float32)
    return pl.pallas_call(
        functools.partial(update_kernel, entries, replicas),
        out_shape=(jax.ShapeDtypeStruct((copies, layers, share, width), jnp.bfloat16), tile, tile),
        in_specs=[pl.BlockSpec(memory_space=pltpu.SMEM)] * 2 + [WHOLE] * 5,
        out_specs=(WHOLE,) * 3,
        compiler_params=VMEM,
    )(layer, outer_step, parts, own, behind, ahead, owned)


def mix_kernel(
    order, alpha_ref, factor_ref, average_ref, momentum_ref, gathered_ref, local_ref,
    new_global_ref, new_momentum_ref, mixed_ref, momentum_tile, mixed_tile, stored, kept, sent,
):
    alpha = alpha_ref[:, 0:1]
    rest = 1.0 - alpha
    factor = factor_ref[:, 0:1]
    columns, layers, _, width = gathered_ref.shape
    copies = []
    for layer in range(layers):
        for i, column in enumerate(order):
            j = layer * columns + column
            copies.append(pltpu.make_async_copy(gathered_ref.at[i, layer], new_global_ref.at[j], kept.at[j]))
            copies[-1].start()
    for start in range(0, width, 1024):
        lanes = pl.ds(start, 1024)
        momentum_tile[:, lanes] = 0.9 * momentum_ref[:, lanes] + factor * average_ref[:, lanes]
    copies.append(pltpu.make_async_copy(momentum_tile, new_momentum_ref, stored))
    copies[-1].start()
    for layer in range(layers):
        for i, column in enumerate(order):
            j = layer * columns + column
            for start in range(0, width, 1024):
                lanes = pl.ds(start, 1024)
                mixed_tile[j, :, lanes] = (
                    alpha * local_ref[j, :, lanes].astype(jnp.float32)
                    + rest * gathered_ref[i, layer, :, lanes].astype(jnp.float32)
                ).astype(jnp.bfloat16)
            copies.append(pltpu.make_async_copy(mixed_tile.at[j], mixed_ref.at[j], sent.at[j]))
            copies[-1].start()
    for copy in copies:
        copy.wait()


def mix(order, alpha, factor, average, momentum, gathered, local_weights):
    columns, layers, share, width = gathered.shape
    count = layers * columns
    shape = jax.ShapeDtypeStruct((count, share, width), jnp.bfloat16)
    far = pl.BlockSpec(memory_space=pl.ANY)
    return pl.pallas_call(
        functools.partial(mix_kernel, order),
        out_shape=(shape, jax.ShapeDtypeStruct(momentum.shape, jnp.float32), shape),
        in_specs=[WHOLE] * 6,
        out_specs=(far,) * 3,
        scratch_shapes=[
            pltpu.VMEM(momentum.shape, jnp.float32),
            pltpu.VMEM(shape.shape, jnp.bfloat16),
            pltpu.SemaphoreType.DMA(()),
            pltpu.SemaphoreType.DMA((count,)),
            pltpu.SemaphoreType.DMA((count,)),
        ],
        compiler_params=VMEM,
    )(alpha, factor, average, momentum, gathered, local_weights.reshape(shape.shape))


def grouped(lengths, inside):
    names = list(lengths)
    strides = {n: 1 for n in names}
    for n, after in zip(names[-2::-1], names[:0:-1]):
        strides[n] = strides[after] * lengths[after]
    outside = [n for n in names if n not in inside]

    def offsets(axes):
        steps = [[i * strides[n] for i in range(lengths[n])] for n in axes]
        return [sum(each) for each in itertools.product(*steps)]

    return [[a + b for b in offsets(inside)] for a in offsets(outside)]


def exchange(copies, groups):
    return lax.all_to_all(copies, ("rep", "fsdp"), 0, 0, tiled=True, axis_index_groups=groups)


def shards(global_weights, local_weights, outer_momentum, outer_step):
    replicas = lax.axis_size("rep")
    peers = lax.axis_size("fsdp")
    rows_dev, width = global_weights.shape
    share = rows_dev // replicas
    lengths = dict(z_lo=3, x=4, y=8, z_hi=4, core=2)
    layers, columns = lengths["z_lo"], lengths["x"]
    place = lax.axis_index("rep")
    owned = lax.dynamic_index_in_dim(
        global_weights.reshape(layers, columns, share, width), lax.rem(place, columns), 1, keepdims=False
    )
    plane = grouped(lengths, ("x", "y"))
    line = grouped(lengths, ("z_lo", "z_hi", "core"))
    decoded = quantize(global_weights, local_weights[0])
    slots = [2 * tile + i for tile in TILES for i in range(2)]
    parts = lax.all_to_all(
        decoded.reshape(replicas, share, width), "rep", 0, 0, tiled=True, axis_index_groups=[slots]
    )
    average, carried, partial = totals(parts, outer_momentum, len(line[0]))
    behind, ahead = (
        lax.ppermute(carried, "rep", [(i, (i + away * columns) % replicas) for i in range(replicas)])
        for away in (1, 2)
    )
    partial = jnp.sum(exchange(partial, line), axis=0)
    partials = exchange(jnp.broadcast_to(partial[None], (len(plane[0]),) + partial.shape), plane)
    entries = float(rows_dev * peers * width)
    layer = (place // columns).astype(jnp.int32)[None]
    copies, alpha, factor = update(
        entries, replicas, layer, outer_step, partials, carried, behind, ahead, owned, columns
    )
    order = (0, 1, 3, 2)
    beside = [[i * columns + j for j in order] for i in range(layers)]
    gathered = lax.all_to_all(copies, "rep", 0, 0, tiled=True, axis_index_groups=beside)
    new_global, new_momentum, mixed_local = mix(
        order, alpha, factor, average, outer_momentum, gathered, local_weights[0]
    )
    return (
        new_global.reshape(rows_dev, width),
        new_momentum,
        mixed_local.reshape(local_weights.shape),
    )


def solution(mesh):
    placed = (P("fsdp", None), P("rep", "fsdp", None), P(("fsdp", "rep"), None), P("rep"))
    return jax.shard_map(
        shards,
        mesh=mesh,
        in_specs=placed,
        out_specs=(P("fsdp", None), P(("fsdp", "rep"), None), P("rep", "fsdp", None)),
        check_vma=False,
    )
```

```python
import functools
import itertools

import jax
import jax.numpy as jnp
from jax import lax
from jax.experimental import pallas as pl
from jax.experimental.pallas import tpu as pltpu
from jax.sharding import PartitionSpec as P

BLOCK = 128
SPLIT = 2.0**23 + 1.0
TILES = (2, 0, 1, 5, 4, 3)
VMEM = pltpu.CompilerParams(vmem_limit_bytes=24 * 2**20)
WHOLE = pl.BlockSpec(memory_space=pltpu.VMEM)


def one_bit(values):
    wide = values * SPLIT
    return wide - (wide - values)


def quantize_kernel(global_ref, local_ref, decoded_ref, global_tile, local_tile, decoded_tile, arrived, sent):
    step = 16
    count = global_ref.shape[0] // step

    def tile_rows(i):
        return pl.ds(pl.multiple_of(i * step, step), step)

    def fetch(i):
        return [
            pltpu.make_async_copy(ref.at[tile_rows(i)], tile.at[tile_rows(i)], arrived.at[k, i])
            for k, (ref, tile) in enumerate(((global_ref, global_tile), (local_ref, local_tile)))
        ]

    def put(i):
        slot = sum(jnp.where(i == tile, s, 0) for s, tile in enumerate(TILES))
        return pltpu.make_async_copy(decoded_tile.at[tile_rows(i)], decoded_ref.at[tile_rows(slot)], sent.at[i])

    for i in range(count):
        for copy in fetch(i):
            copy.start()

    @pl.loop(0, count)
    def _(i):
        for copy in fetch(i):
            copy.wait()
        for start in range(0, global_ref.shape[1], BLOCK):
            at = (tile_rows(i), pl.ds(start, BLOCK))
            delta = global_tile[at].astype(jnp.float32) - local_tile[at].astype(jnp.float32)
            magnitude = jnp.abs(delta)
            largest = jnp.maximum(jnp.max(magnitude, axis=1, keepdims=True), 2.0**-24)
            scale = jnp.minimum(one_bit(largest * (1.5 - 2.0**-23)), 2.0**15)
            least = scale * 2.0**-7
            level = jnp.maximum(one_bit(magnitude), least + least)
            level = jnp.where(magnitude >= least, level, 0.0)
            decoded_tile[at] = jnp.where(delta < 0.0, -level, level).astype(jnp.bfloat16)
        put(i).start()

    for i in range(count):
        put(i).wait()


def quantize(global_weights, local_weights):
    shape = global_weights.shape
    far = pl.BlockSpec(memory_space=pl.ANY)
    steps = shape[0] // 16
    return pl.pallas_call(
        quantize_kernel,
        out_shape=jax.ShapeDtypeStruct(shape, jnp.bfloat16),
        in_specs=[far, far],
        out_specs=far,
        scratch_shapes=[
            pltpu.VMEM(shape, jnp.bfloat16),
            pltpu.VMEM(shape, jnp.bfloat16),
            pltpu.VMEM(shape, jnp.bfloat16),
            pltpu.SemaphoreType.DMA((2, steps)),
            pltpu.SemaphoreType.DMA((steps,)),
        ],
    )(global_weights, local_weights)


def total_kernel(parts_ref, momentum_ref, average_ref, carried_ref, squares_ref):
    squares = jnp.zeros((parts_ref.shape[1], BLOCK), jnp.float32)
    for start in range(0, parts_ref.shape[2], BLOCK):
        lanes = pl.ds(start, BLOCK)
        total = parts_ref[0, :, lanes].astype(jnp.float32)
        for r in range(1, parts_ref.shape[0]):
            total += parts_ref[r, :, lanes].astype(jnp.float32)
        average = total / parts_ref.shape[0]
        average_ref[:, lanes] = average
        squares += average * average
        momentum = momentum_ref[:, lanes]
        coarse = momentum.astype(jnp.bfloat16)
        carried_ref[0, :, lanes] = total.astype(jnp.bfloat16)
        carried_ref[1, :, lanes] = coarse
        carried_ref[2, :, lanes] = (momentum - coarse.astype(jnp.float32)).astype(jnp.bfloat16)
    squares = jnp.sum(squares, axis=0, keepdims=True)
    for i in range(squares_ref.shape[0]):
        squares_ref[i] = squares


def totals(parts, momentum, copies):
    share, width = momentum.shape
    return pl.pallas_call(
        total_kernel,
        out_shape=(
            jax.ShapeDtypeStruct((share, width), jnp.float32),
            jax.ShapeDtypeStruct((3, share, width), jnp.bfloat16),
            jax.ShapeDtypeStruct((copies, 1, BLOCK), jnp.float32),
        ),
        in_specs=[WHOLE, WHOLE],
        out_specs=(WHOLE, WHOLE, WHOLE),
        compiler_params=VMEM,
    )(parts, momentum)


def update_kernel(
    entries, replicas, layer_ref, step_ref, parts_ref, own_ref, behind_ref, ahead_ref, owned_ref,
    copies_ref, alpha_ref, factor_ref,
):
    steps = jnp.full(alpha_ref.shape, step_ref[0], jnp.int32).astype(jnp.float32)
    alpha_ref[...] = 0.9 / (1.0 + 0.1 * steps)
    squares = jnp.sum(jnp.sum(parts_ref[...], axis=0), keepdims=True)
    factor = 0.5 / jnp.sqrt(squares / entries + 1e-06)
    part = factor / replicas
    factor_ref[...] = jnp.broadcast_to(factor, factor_ref.shape)
    layers = owned_ref.shape[0]
    step = 512
    for away, carried_ref in enumerate((own_ref, behind_ref, ahead_ref)):
        layer = lax.rem(layer_ref[0] + layers - away, layers)
        for start in range(0, own_ref.shape[2], step):
            lanes = pl.ds(start, step)
            total, coarse, fine = (carried_ref[i, :, lanes].astype(jnp.float32) for i in range(3))
            clipped = part * total
            new_momentum = 0.9 * (coarse + fine) + clipped
            share = (
                owned_ref[layer, :, lanes].astype(jnp.float32) - 0.7 * (clipped + 0.9 * new_momentum)
            ).astype(jnp.bfloat16)
            for i in range(copies_ref.shape[0]):
                copies_ref[i, layer, :, lanes] = share


def update(entries, replicas, layer, outer_step, parts, own, behind, ahead, owned, copies):
    layers, share, width = owned.shape
    tile = jax.ShapeDtypeStruct((share, BLOCK), jnp.float32)
    return pl.pallas_call(
        functools.partial(update_kernel, entries, replicas),
        out_shape=(jax.ShapeDtypeStruct((copies, layers, share, width), jnp.bfloat16), tile, tile),
        in_specs=[pl.BlockSpec(memory_space=pltpu.SMEM)] * 2 + [WHOLE] * 5,
        out_specs=(WHOLE,) * 3,
        compiler_params=VMEM,
    )(layer, outer_step, parts, own, behind, ahead, owned)


def mix_kernel(
    order, alpha_ref, factor_ref, average_ref, momentum_ref, gathered_ref, local_ref,
    new_global_ref, new_momentum_ref, mixed_ref, momentum_tile, mixed_tile, stored, kept, sent,
):
    alpha = alpha_ref[:, 0:1]
    rest = 1.0 - alpha
    factor = factor_ref[:, 0:1]
    columns, layers, _, width = gathered_ref.shape
    copies = []
    for layer in range(layers):
        for i, column in enumerate(order):
            j = layer * columns + column
            copies.append(pltpu.make_async_copy(gathered_ref.at[i, layer], new_global_ref.at[j], kept.at[j]))
            copies[-1].start()
    for start in range(0, width, 1024):
        lanes = pl.ds(start, 1024)
        momentum_tile[:, lanes] = 0.9 * momentum_ref[:, lanes] + factor * average_ref[:, lanes]
    copies.append(pltpu.make_async_copy(momentum_tile, new_momentum_ref, stored))
    copies[-1].start()
    for layer in range(layers):
        for i, column in enumerate(order):
            j = layer * columns + column
            for start in range(0, width, 1024):
                lanes = pl.ds(start, 1024)
                mixed_tile[j, :, lanes] = (
                    alpha * local_ref[j, :, lanes].astype(jnp.float32)
                    + rest * gathered_ref[i, layer, :, lanes].astype(jnp.float32)
                ).astype(jnp.bfloat16)
            copies.append(pltpu.make_async_copy(mixed_tile.at[j], mixed_ref.at[j], sent.at[j]))
            copies[-1].start()
    for copy in copies:
        copy.wait()


def mix(order, alpha, factor, average, momentum, gathered, local_weights):
    columns, layers, share, width = gathered.shape
    count = layers * columns
    shape = jax.ShapeDtypeStruct((count, share, width), jnp.bfloat16)
    far = pl.BlockSpec(memory_space=pl.ANY)
    return pl.pallas_call(
        functools.partial(mix_kernel, order),
        out_shape=(shape, jax.ShapeDtypeStruct(momentum.shape, jnp.float32), shape),
        in_specs=[WHOLE] * 6,
        out_specs=(far,) * 3,
        scratch_shapes=[
            pltpu.VMEM(momentum.shape, jnp.float32),
            pltpu.VMEM(shape.shape, jnp.bfloat16),
            pltpu.SemaphoreType.DMA(()),
            pltpu.SemaphoreType.DMA((count,)),
            pltpu.SemaphoreType.DMA((count,)),
        ],
        compiler_params=VMEM,
    )(alpha, factor, average, momentum, gathered, local_weights.reshape(shape.shape))


def grouped(lengths, inside):
    names = list(lengths)
    strides = {n: 1 for n in names}
    for n, after in zip(names[-2::-1], names[:0:-1]):
        strides[n] = strides[after] * lengths[after]
    outside = [n for n in names if n not in inside]

    def offsets(axes):
        steps = [[i * strides[n] for i in range(lengths[n])] for n in axes]
        return [sum(each) for each in itertools.product(*steps)]

    return [[a + b for b in offsets(inside)] for a in offsets(outside)]


def exchange(copies, groups):
    return lax.all_to_all(copies, ("rep", "fsdp"), 0, 0, tiled=True, axis_index_groups=groups)


def shards(global_weights, local_weights, outer_momentum, outer_step):
    replicas = lax.axis_size("rep")
    peers = lax.axis_size("fsdp")
    rows_dev, width = global_weights.shape
    share = rows_dev // replicas
    lengths = dict(z_lo=3, x=4, y=8, z_hi=4, core=2)
    layers, columns = lengths["z_lo"], lengths["x"]
    place = lax.axis_index("rep")
    owned = lax.dynamic_index_in_dim(
        global_weights.reshape(layers, columns, share, width), lax.rem(place, columns), 1, keepdims=False
    )
    plane = grouped(lengths, ("x", "y"))
    line = grouped(lengths, ("z_lo", "z_hi", "core"))
    decoded = quantize(global_weights, local_weights[0])
    slots = [2 * tile + i for tile in TILES for i in range(2)]
    parts = lax.all_to_all(
        decoded.reshape(replicas, share, width), "rep", 0, 0, tiled=True, axis_index_groups=[slots]
    )
    average, carried, partial = totals(parts, outer_momentum, len(line[0]))
    behind, ahead = (
        lax.ppermute(carried, "rep", [(i, (i + away * columns) % replicas) for i in range(replicas)])
        for away in (1, 2)
    )
    partial = jnp.sum(exchange(partial, line), axis=0)
    partials = exchange(jnp.broadcast_to(partial[None], (len(plane[0]),) + partial.shape), plane)
    entries = float(rows_dev * peers * width)
    layer = (place // columns).astype(jnp.int32)[None]
    copies, alpha, factor = update(
        entries, replicas, layer, outer_step, partials, carried, behind, ahead, owned, columns
    )
    order = (0, 1, 3, 2)
    beside = [[i * columns + j for j in order] for i in range(layers)]
    gathered = lax.all_to_all(copies, "rep", 0, 0, tiled=True, axis_index_groups=beside)
    new_global, new_momentum, mixed_local = mix(
        order, alpha, factor, average, outer_momentum, gathered, local_weights[0]
    )
    return (
        new_global.reshape(rows_dev, width),
        new_momentum,
        mixed_local.reshape(local_weights.shape),
    )


def solution(mesh):
    placed = (P("fsdp", None), P("rep", "fsdp", None), P(("fsdp", "rep"), None), P("rep"))
    return jax.shard_map(
        shards,
        mesh=mesh,
        in_specs=placed,
        out_specs=(P("fsdp", None), P(("fsdp", "rep"), None), P("rep", "fsdp", None)),
        check_vma=False,
    )
```
